512 devices in a mesh: dp: 64 (over y, z), fsdp: 8 (over x, core).
Axes of the slice: x: 4, y: 8, z: 8, core: 2. Of those that a mesh axis runs over, the one named last changes fastest.
Arguments:
- teacher_feat: bfloat16 [16384, 256], P(('dp', 'fsdp')), may hold values from -1 to 1
- student_feat: bfloat16 [16384, 256], P(('dp', 'fsdp')), may hold values from -1 to 1
- crop_weight: bfloat16 [16384], P(('dp', 'fsdp')), may hold values from -96 to 96
- teacher_v: bfloat16 [256, 32768], P(None, 'fsdp'), may hold values from -2 to 2
- student_v: bfloat16 [256, 32768], P(None, 'fsdp'), may hold values from -2 to 2
Outputs:
- grad_v: float32 [256, 32768], P('dp', 'fsdp')
- grad_feat: float32 [16384, 256], P(('dp', 'fsdp'))
The draws below stay inside these ranges and needn't reach their ends.
All inputs are finite; a program needn't handle non-finite values.
Results may differ from the reference program's by a relative error of at most 0.0073.
Values may be sent and summed in bfloat16 or wider, within the bound.
A program may use at most 64 MiB of HBM per device.

```python
import jax
import jax.numpy as jnp
from jax import lax

BOT = 256
K = 32768
ITERS = 3
CROPS = 16384


groups = 8


def directions(key):
    return jnp.clip(jax.random.normal(jax.random.fold_in(key, 100), (groups, BOT), jnp.float32), -4.0, 4.0)


def crop_groups(key):
    levels = jax.random.randint(jax.random.fold_in(key, 101), (CROPS,), 1, 256)
    counted = jnp.zeros((CROPS,), jnp.int32)
    for exponent in range(1, groups):
        counted = counted + (levels >= 2 ** exponent).astype(jnp.int32)
    return counted


def prototype_groups(key):
    return jax.random.randint(jax.random.fold_in(key, 102), (K,), 0, groups)


def crop_shared(key):
    return jnp.take(directions(key), crop_groups(key), axis=0)


def prototype_shared(key):
    return jnp.transpose(jnp.take(directions(key), prototype_groups(key), axis=0))


def draw_teacher_feat(key, part):
    shared = crop_shared(key)
    key = jax.random.fold_in(key, 3)
    jitter = jnp.clip(jax.random.normal(key, (CROPS, BOT), jnp.float32), -4.0, 4.0)
    values = 0.5 * shared + jitter
    return (0.0625 * values).astype(jnp.bfloat16)


def draw_student_feat(key, part):
    shared = crop_shared(key)
    key = jax.random.fold_in(key, 4)
    jitter = jnp.clip(jax.random.normal(key, (CROPS, BOT), jnp.float32), -4.0, 4.0)
    values = 0.6 * shared + jitter
    return (0.0625 * values).astype(jnp.bfloat16)


def draw_teacher_v(key, part):
    shared = prototype_shared(key)
    key = jax.random.fold_in(key, 5)
    jitter = jnp.clip(jax.random.normal(key, (BOT, K), jnp.float32), -4.0, 4.0)
    values = 0.5 * shared + jitter
    return (values * BOT ** (-0.5)).astype(jnp.bfloat16)


def draw_student_v(key, part):
    shared = prototype_shared(key)
    key = jax.random.fold_in(key, 6)
    position = jnp.arange(K).astype(jnp.float32)[None, :] / K
    jitter = jnp.clip(jax.random.normal(key, (BOT, K), jnp.float32), -4.0, 4.0)
    values = 2.0 * position * shared + jitter
    return jnp.clip(values * BOT ** (-0.5), -2.0, 2.0).astype(jnp.bfloat16)


def block_scale(stream_key, shape, pieces, low, largest):
    loudness = 1.0
    for dim, blocks in pieces:
        steps = jax.random.uniform(jax.random.fold_in(jax.random.fold_in(stream_key, 6), dim), (blocks,), jnp.float32, low / len(pieces), largest / len(pieces))
        loudness = loudness * jnp.repeat(jnp.exp(steps), shape[dim] // blocks).reshape((-1,) + (1,) * (len(shape) - 1 - dim))
    return loudness


def bell_draw(stream_key, dims, width, limit, cuts=(), dtype=jnp.bfloat16):
    loudness = block_scale(stream_key, dims, cuts, -0.22, 0.18) if cuts else 1.0
    result = jax.random.normal(stream_key, dims, jnp.float32) * width * loudness
    return jnp.minimum(jnp.maximum(result, -limit), limit).astype(dtype)


def setup_inputs(seed: int = 0) -> dict:
    key_of = jax.random.split(jax.random.key(seed), 6)
    teacher_feat = draw_teacher_feat(jax.random.fold_in(key_of[5], 71), 0)
    student_feat = draw_student_feat(jax.random.fold_in(key_of[5], 71), 0)
    crop_weight = bell_draw(key_of[2], (CROPS,), 16.0, 96.0, ((0, 512),))
    teacher_v = draw_teacher_v(jax.random.fold_in(key_of[5], 71), 0)
    student_v = draw_student_v(jax.random.fold_in(key_of[5], 71), 0)
    return {"teacher_feat": teacher_feat, "student_feat": student_feat, "crop_weight": crop_weight, "teacher_v": teacher_v, "student_v": student_v}


teacher_temp = 0.04
student_temp = 0.1
epsilon = 1e-06
block_rows = 512

def unit_rows(values):
    floats = values.astype(jnp.float32)
    length = jnp.sqrt(lax.optimization_barrier(jnp.sum(floats * floats, axis=1, keepdims=True)) + epsilon)
    return (floats / length, length)

def unit_columns(values):
    floats = values.astype(jnp.float32)
    length = jnp.sqrt(lax.optimization_barrier(jnp.sum(floats * floats, axis=0, keepdims=True)) + epsilon)
    return (floats / length, length)

def reference(teacher_feat, student_feat, crop_weight, teacher_v, student_v):
    teacher_hat, _ = unit_rows(teacher_feat)
    student_hat, student_len = unit_rows(student_feat)
    teacher_w, _ = unit_columns(teacher_v)
    student_w, student_wlen = unit_columns(student_v)
    teacher_wunit = teacher_w.astype(jnp.bfloat16)
    student_wunit = student_w.astype(jnp.bfloat16)
    blocks = max(CROPS // block_rows, 1)
    rows_each = CROPS // blocks
    teacher_blocks = teacher_hat.astype(jnp.bfloat16).reshape(blocks, rows_each, BOT)
    student_blocks = student_hat.astype(jnp.bfloat16).reshape(blocks, rows_each, BOT)
    weight_blocks = crop_weight.astype(jnp.float32).reshape(blocks, rows_each)

    def teacher_mass(rows_teacher):
        return jnp.exp(jnp.dot(rows_teacher, teacher_wunit, preferred_element_type=jnp.float32) / teacher_temp)
    row_scale = jnp.ones((blocks, rows_each), jnp.float32)
    col_scale = jnp.ones((K,), jnp.float32)
    for sweep_index in range(ITERS):

        def add_columns(running, inputs):
            rows_teacher, scale_rows = inputs
            mass = teacher_mass(rows_teacher) * scale_rows[:, None] * col_scale[None, :]
            return (running + lax.optimization_barrier(jnp.sum(mass, axis=0)), None)
        proto_mass, _ = lax.scan(add_columns, jnp.zeros((K,), jnp.float32), (teacher_blocks, row_scale))
        col_scale = col_scale / (proto_mass * K)

        def sum_rows(inputs):
            rows_teacher, scale_rows = inputs
            mass = teacher_mass(rows_teacher) * scale_rows[:, None] * col_scale[None, :]
            return lax.optimization_barrier(jnp.sum(mass, axis=1))
        crop_mass = lax.map(sum_rows, (teacher_blocks, row_scale))
        row_scale = row_scale / (crop_mass * CROPS)

    def backward(running, inputs):
        rows_teacher, rows_student, scale_rows, weight_rows = inputs
        target = teacher_mass(rows_teacher) * scale_rows[:, None] * col_scale[None, :] * CROPS
        student_mass = jnp.exp(jnp.dot(rows_student, student_wunit, preferred_element_type=jnp.float32) / student_temp)
        student_prob = student_mass / lax.optimization_barrier(jnp.sum(student_mass, axis=1, keepdims=True))
        gradient = ((student_prob - target) * weight_rows[:, None] / student_temp).astype(jnp.bfloat16)
        running = running + lax.dot_general(rows_student, gradient, (((0,), (0,)), ((), ())), preferred_element_type=jnp.float32)
        feature_part = lax.dot_general(gradient, student_wunit, (((1,), (1,)), ((), ())), preferred_element_type=jnp.float32)
        return (running, feature_part)
    weight_grad, feature_grad = lax.scan(backward, jnp.zeros((BOT, K), jnp.float32), (teacher_blocks, student_blocks, row_scale, weight_blocks))
    feature_grad = feature_grad.reshape(CROPS, BOT)
    grad_feat = (feature_grad - student_hat * lax.optimization_barrier(jnp.sum(student_hat * feature_grad, axis=1, keepdims=True))) / student_len
    grad_v = (weight_grad - student_w * lax.optimization_barrier(jnp.sum(student_w * weight_grad, axis=0, keepdims=True))) / student_wlen
    return (grad_v, grad_feat)
```

```python
import functools

import jax
import jax.numpy as jnp
from jax import lax
from jax.experimental import pallas as pl
from jax.experimental.pallas import tpu as pltpu
from jax.sharding import PartitionSpec as P

K = 32768
ITERS = 3
BLOCKS = 16
HALF = BLOCKS // 2

teacher_temp = 0.04
student_temp = 0.1
epsilon = 1e-06
F32 = jnp.float32
BF16 = jnp.bfloat16
MESH = pl.DeviceIdType.MESH


def far_first(n):
    return sorted(range(1, n), key=lambda j: -min(j, n - j))


def lanes_of(partial):
    return jnp.sum(jnp.transpose(partial), axis=0, keepdims=True)


def rows_of(vector, width):
    return jnp.transpose(jnp.broadcast_to(vector, (width, vector.shape[1])))


def dot_nt(a, b):
    return lax.dot_general(a, b, (((1,), (1,)), ((), ())), preferred_element_type=F32)


def dot_nn(a, b):
    return jnp.dot(a, b, preferred_element_type=F32)


def kernel(
    geo,
    tf_hbm, sf_hbm, cw_ref, tv_hbm, sv_hbm,
    gv_ref, gf_ref,
    tf, sf, tv, sv, sw, tu, su, sut, perm, mass, prob, winv, svec, rb, ab, bb, fg,
    col_own, col_recv, row_own, row_recv, st_own, st_recv,
    part, ring_recv, second, second_recv, fg_recv,
    local_sem, gather_send, gather_recv, col_send, col_got, row_send, row_got, st_send, st_got,
    ring_send, ring_got, second_send, second_got, fg_send, fg_got,
):
    ny, nz, nf = geo
    local = tf.shape[0]
    bot = tv.shape[0]
    kl = tv.shape[1]
    rows = local * nf
    cb = kl // BLOCKS
    crops = rows * ny * nz
    protos = kl * nf
    dp, f = lax.axis_index("dp"), lax.axis_index("fsdp")
    y, z = dp // nz, lax.rem(dp, nz)

    def on_y(j):
        return {"dp": lax.rem(y + j, ny) * nz + z}

    def on_z(j):
        return {"dp": y * nz + lax.rem(z + j, nz)}

    def on_f(j):
        return {"fsdp": lax.rem(f + j, nf)}

    axes = ((on_y, ny, y), (on_z, nz, z))

    def block(j):
        return pl.ds(pl.multiple_of(j * cb, cb), cb)

    def send(src, dst, send_sem, recv_sem, device):
        pltpu.make_async_remote_copy(
            src_ref=src, dst_ref=dst, send_sem=send_sem, recv_sem=recv_sem,
            device_id=device, device_id_type=MESH,
        ).start()

    def took(ref, sem):
        pltpu.make_async_copy(ref, ref, sem).wait()

    loads = [
        pltpu.make_async_copy(src, dst, local_sem.at[i])
        for i, (src, dst) in enumerate(((tf_hbm, tf), (sf_hbm, sf), (tv_hbm, tv), (sv_hbm, sv)))
    ]
    for load in loads:
        load.start()
    barrier = pltpu.get_barrier_semaphore()
    for axis, n in ((on_f, nf), (on_y, ny), (on_z, nz)):
        for j in far_first(n):
            pl.semaphore_signal(barrier, inc=1, device_id=axis(j), device_id_type=MESH)

    own = pl.ds(pl.multiple_of(f * local, local), local)

    def unit_rows(ref):
        values = ref[...].astype(F32)
        length = jnp.sqrt(jnp.sum(values * values, axis=1, keepdims=True) + epsilon)
        return values / length, length

    loads[0].wait()
    tu[own, :] = unit_rows(tf)[0].astype(BF16)
    loads[1].wait()
    su[own, :] = unit_rows(sf)[0].astype(BF16)
    pl.semaphore_wait(barrier, nf + ny + nz - 3)
    for i, unit in enumerate((tu, su)):
        for j in far_first(nf):
            send(unit.at[own], unit.at[own], gather_send.at[i], gather_recv.at[i], on_f(j))
    others = pl.ds(0, rows - local)

    loads[2].wait()

    @pl.loop(0, BLOCKS)
    def _(j):
        values = tv[:, block(j)].astype(F32)
        inverse = 1.0 / jnp.sqrt(jnp.sum(values * values, axis=0, keepdims=True) + epsilon)
        tv[:, block(j)] = (values * inverse).astype(BF16)

    def student_prototypes():
        loads[3].wait()

        @pl.loop(0, BLOCKS)
        def _(j):
            values = sv[:, block(j)].astype(F32)
            inverse = 1.0 / jnp.sqrt(jnp.sum(values * values, axis=0, keepdims=True) + epsilon)
            winv[pl.ds(j, 1), :] = inverse
            sw[:, block(j)] = (values * inverse).astype(BF16)

    def student_orders():
        each = bot // (ny * nz)
        p = lax.broadcasted_iota(jnp.int32, (bot, bot), 0)
        d = lax.broadcasted_iota(jnp.int32, (bot, bot), 1)
        pz, py, pi = p // (ny * each), lax.rem(p // each, ny), lax.rem(p, each)
        perm[...] = (d == (py * nz + pz) * each + pi).astype(F32).astype(BF16)
        took(su.at[others], gather_recv.at[1])
        units = su[...]
        sut[0] = dot_nt((d == p).astype(F32).astype(BF16), units).astype(BF16)
        sut[1] = dot_nt(perm[...], units).astype(BF16)

        @pl.loop(HALF, BLOCKS)
        def _(j):
            sv[:, block(j)] = dot_nn(perm[...], sv[:, block(j)]).astype(BF16)

    def student_mass():
        def step(j, total):
            values = jnp.exp(dot_nn(su[...], sw[:, block(j)]) * (1.0 / student_temp))
            prob[j] = values
            for c in range(0, cb, 128):
                total = total + values[:, c : c + 128]
            return total

        total = lax.fori_loop(0, BLOCKS, step, jnp.zeros((rows, 128), F32))
        st_own[0] = lanes_of(total)
        i = lax.broadcasted_iota(jnp.int32, (local, rows), 0)
        c = lax.broadcasted_iota(jnp.int32, (local, rows), 1)
        place = (c == f * local + i).astype(F32).astype(BF16)
        st_own[1] = dot_nn(cw_ref[...], place)
        for j in far_first(nf):
            send(st_own, st_recv.at[j - 1], st_send, st_got, on_f(j))

    def col_first(it, h):
        axis, n, _ = axes[h]
        for j in far_first(n):
            send(col_own.at[it, h, 0], col_recv.at[it, h, 0, j - 1], col_send.at[it, h, 0], col_got.at[it, h, 0], axis(j))

    def col_total(it, h, stage):
        n = axes[(h + stage) % 2][1]
        took(col_recv.at[it, h, stage], col_got.at[it, h, stage])
        total = col_own[it, h, stage]
        for j in range(n - 1):
            total = total + col_recv[it, h, stage, j]
        return total

    def col_second(it, h):
        col_own[it, h, 1] = col_total(it, h, 0)
        axis, n, _ = axes[1 - h]
        for j in far_first(n):
            send(col_own.at[it, h, 1], col_recv.at[it, h, 1, j - 1], col_send.at[it, h, 1], col_got.at[it, h, 1], axis(j))

    took(tu.at[others], gather_recv.at[0])
    for it in range(ITERS):
        for h in range(2):

            @pl.loop(0, HALF)
            def _(k):
                j = h * HALF + k
                if it == 0:
                    values = jnp.exp(dot_nn(tu[...], tv[:, block(j)]) * (1.0 / teacher_temp))
                    mass[j] = values
                else:
                    values = mass[j] * rb[...]
                col_own[it, h, 0, pl.ds(k, 1), :] = jnp.sum(values, axis=0, keepdims=True)

            col_first(it, h)
        if it == 0:
            student_prototypes()
        if it == 1:
            student_mass()
        for h in range(2):
            col_second(it, h)
        if it == 0:
            student_orders()
        total = jnp.zeros((rows, 128), F32)
        for h in range(2):
            svec[h * HALF : (h + 1) * HALF, :] = 1.0 / (col_total(it, h, 1) * protos)

            def row_step(k, total):
                j = h * HALF + k
                values = mass[j] * svec[pl.ds(j, 1), :]
                for c in range(0, cb, 128):
                    total = total + values[:, c : c + 128]
                return total

            total = lax.fori_loop(0, HALF, row_step, total)
        row_own[it] = lanes_of(total)
        for j in far_first(nf):
            send(row_own.at[it], row_recv.at[it, j - 1], row_send.at[it], row_got.at[it], on_f(j))
        if it == ITERS - 1:
            took(st_recv, st_got)
            student_total, weights = st_own[0], st_own[1]
            for j in range(nf - 1):
                student_total = student_total + st_recv[j, 0]
                weights = weights + st_recv[j, 1]
            ab[...] = rows_of(weights / (student_total * student_temp), cb)
        took(row_recv.at[it], row_got.at[it])
        row_total = row_own[it]
        for j in range(nf - 1):
            row_total = row_total + row_recv[it, j]
        if it < ITERS - 1:
            rb[...] = rows_of(1.0 / (row_total * crops), cb)
        else:
            bb[...] = rows_of(weights / (row_total * student_temp), cb)

    fg[...] = jnp.zeros_like(fg)
    rings = [(h, way, sub) for sub in range(2) for way in range(2) for h in range(2)]

    def ring_id(h, way, sub):
        return h * 4 + way * 2 + sub

    def chunk(h, c):
        size = bot // axes[h][1]
        return pl.ds(pl.multiple_of(c * size, size), size)

    def ring_step(h, way, sub, s):
        axis, n, me = axes[h]
        r = ring_id(h, way, sub)
        ahead = 1 if way == 0 else n - 1
        c = lax.rem(me + (n - 1 - s if way == 0 else 1 + s), n)
        if s > 0:
            took(ring_recv.at[r, s - 1], ring_got.at[r, s - 1])
            part[r, chunk(h, c), :] = part[r, chunk(h, c), :] + ring_recv[r, s - 1]
        send(part.at[r, chunk(h, c)], ring_recv.at[r, s], ring_send.at[r], ring_got.at[r, s], axis(ahead))

    for h, way, sub in rings:
        r = ring_id(h, way, sub)
        for k in range(2):
            j = 2 * r + k
            g = (prob[j] * ab[...] - mass[j] * bb[...] * svec[j : j + 1, :]).astype(BF16)
            columns = slice(j * cb, (j + 1) * cb)
            fg[...] += dot_nt(g, sw[:, columns])
            grad = dot_nn(sut[h], g)
            inverse = winv[j : j + 1, :]
            w = sv[:, columns].astype(F32) * inverse
            inner = jnp.sum(w * grad, axis=0, keepdims=True)
            part[r, :, k * cb : (k + 1) * cb] = ((grad - w * inner) * inverse).astype(BF16)
        ring_step(h, way, sub, 0)

    def rows_at(i):
        return pl.ds(pl.multiple_of(i * local, local), local)

    for j in far_first(nf):
        send(fg.at[rows_at(lax.rem(f + j, nf))], fg_recv.at[j - 1], fg_send, fg_got, on_f(j))
    for s in range(1, max(ny, nz) - 1):
        for h, way, sub in rings:
            if s < axes[h][1] - 1:
                ring_step(h, way, sub, s)

    each = bot // (ny * nz)
    for h in range(2):
        _, n, me = axes[h]
        sums = []
        for way in range(2):
            for sub in range(2):
                r = ring_id(h, way, sub)
                took(ring_recv.at[r, n - 2], ring_got.at[r, n - 2])
                sums.append(part[r, chunk(h, me), :].astype(F32) + ring_recv[r, n - 2].astype(F32))
        axis, n2, me2 = axes[1 - h]
        for c in range(n2):
            second[h, c] = jnp.concatenate([total[c * each : (c + 1) * each] for total in sums], axis=0).astype(BF16)
        for j in far_first(n2):
            send(second.at[h, lax.rem(me2 + j, n2)], second_recv.at[h, j - 1], second_send.at[h], second_got.at[h], axis(j))

    took(fg_recv, fg_got)
    grad = fg[rows_at(f), :]
    for j in range(nf - 1):
        grad = grad + fg_recv[j]
    hat, length = unit_rows(sf)
    gf_ref[...] = (grad - hat * jnp.sum(hat * grad, axis=1, keepdims=True)) / length

    for h in range(2):
        took(second_recv.at[h], second_got.at[h])
        _, n2, me2 = axes[1 - h]
        total = second[h, me2].astype(F32)
        for j in range(n2 - 1):
            total = total + second_recv[h, j].astype(F32)
        for q in range(4):
            first = h * HALF * cb + q * 2 * cb
            gv_ref[:, first : first + 2 * cb] = total[q * each : (q + 1) * each]

    for i, unit in enumerate((tu, su)):
        took(unit.at[others], gather_send.at[i])
    for it in range(ITERS):
        for h in range(2):
            for stage in range(2):
                took(col_recv.at[it, h, stage], col_send.at[it, h, stage])
        took(row_recv.at[it], row_send.at[it])
    took(st_recv, st_send)
    took(fg_recv, fg_send)
    for h in range(2):
        for way in range(2):
            for sub in range(2):
                r = ring_id(h, way, sub)
                took(ring_recv.at[r], ring_send.at[r])
        took(second_recv.at[h], second_send.at[h])


def step(geo, teacher_feat, student_feat, crop_weight, teacher_v, student_v):
    ny, nz, nf = geo
    local, bot = teacher_feat.shape
    kl = teacher_v.shape[1]
    rows, cb = local * nf, kl // BLOCKS
    each = bot // (ny * nz)
    any_space = pl.BlockSpec(memory_space=pl.ANY)
    vmem = pl.BlockSpec(memory_space=pltpu.VMEM)
    dma = pltpu.SemaphoreType.DMA
    return pl.pallas_call(
        functools.partial(kernel, geo),
        out_shape=(
            jax.ShapeDtypeStruct((each, kl), F32),
            jax.ShapeDtypeStruct((local, bot), F32),
        ),
        in_specs=[any_space, any_space, vmem, any_space, any_space],
        out_specs=(vmem, vmem),
        scratch_shapes=[
            pltpu.VMEM((local, bot), BF16),
            pltpu.VMEM((local, bot), BF16),
            pltpu.VMEM((bot, kl), BF16),
            pltpu.VMEM((bot, kl), BF16),
            pltpu.VMEM((bot, kl), BF16),
            pltpu.VMEM((rows, bot), BF16),
            pltpu.VMEM((rows, bot), BF16),
            pltpu.VMEM((2, bot, rows), BF16),
            pltpu.VMEM((bot, bot), BF16),
            pltpu.VMEM((BLOCKS, rows, cb), F32),
            pltpu.VMEM((BLOCKS, rows, cb), F32),
            pltpu.VMEM((BLOCKS, cb), F32),
            pltpu.VMEM((BLOCKS, cb), F32),
            pltpu.VMEM((rows, cb), F32),
            pltpu.VMEM((rows, cb), F32),
            pltpu.VMEM((rows, cb), F32),
            pltpu.VMEM((rows, bot), F32),
            pltpu.VMEM((ITERS, 2, 2, HALF, cb), F32),
            pltpu.VMEM((ITERS, 2, 2, ny - 1, HALF, cb), F32),
            pltpu.VMEM((ITERS, 1, rows), F32),
            pltpu.VMEM((ITERS, nf - 1, 1, rows), F32),
            pltpu.VMEM((2, 1, rows), F32),
            pltpu.VMEM((nf - 1, 2, 1, rows), F32),
            pltpu.VMEM((8, bot, 2 * cb), BF16),
            pltpu.VMEM((8, ny - 1, bot // ny, 2 * cb), BF16),
            pltpu.VMEM((2, ny, 4 * each, 2 * cb), BF16),
            pltpu.VMEM((2, ny - 1, 4 * each, 2 * cb), BF16),
            pltpu.VMEM((nf - 1, local, bot), F32),
            dma((4,)),
            dma((2,)), dma((2,)),
            dma((ITERS, 2, 2)), dma((ITERS, 2, 2)),
            dma((ITERS,)), dma((ITERS,)),
            dma, dma,
            dma((8,)), dma((8, ny - 1)),
            dma((2,)), dma((2,)),
            dma, dma,
        ],
        compiler_params=pltpu.CompilerParams(
            collective_id=0, has_side_effects=True, vmem_limit_bytes=48 * 1024 * 1024
        ),
    )(teacher_feat, student_feat, crop_weight.reshape(1, local), teacher_v, student_v)


def solution(mesh, planes=(8, 8)):
    geo = (*planes, mesh.shape["fsdp"])
    placed = (
        P(("dp", "fsdp"), None),
        P(("dp", "fsdp"), None),
        P(("dp", "fsdp")),
        P(None, "fsdp"),
        P(None, "fsdp"),
    )
    return jax.shard_map(
        functools.partial(step, geo),
        mesh=mesh,
        in_specs=placed,
        out_specs=(P("dp", "fsdp"), P(("dp", "fsdp"), None)),
        check_vma=False,
    )
```

```python
import functools

import jax
import jax.numpy as jnp
from jax import lax
from jax.experimental import pallas as pl
from jax.experimental.pallas import tpu as pltpu
from jax.sharding import PartitionSpec as P

K = 32768
ITERS = 3
BLOCKS = 16
HALF = BLOCKS // 2

teacher_temp = 0.04
student_temp = 0.1
epsilon = 1e-06
F32 = jnp.float32
BF16 = jnp.bfloat16
MESH = pl.DeviceIdType.MESH


def far_first(n):
    return sorted(range(1, n), key=lambda j: -min(j, n - j))


def lanes_of(partial):
    return jnp.sum(jnp.transpose(partial), axis=0, keepdims=True)


def rows_of(vector, width):
    return jnp.transpose(jnp.broadcast_to(vector, (width, vector.shape[1])))


def dot_nt(a, b):
    return lax.dot_general(a, b, (((1,), (1,)), ((), ())), preferred_element_type=F32)


def dot_nn(a, b):
    return jnp.dot(a, b, preferred_element_type=F32)


def kernel(
    geo,
    tf_hbm, sf_hbm, cw_ref, tv_hbm, sv_hbm,
    gv_ref, gf_ref,
    tf, sf, tv, sv, sw, tu, su, sut, perm, mass, prob, winv, svec, rb, ab, bb, fg,
    col_own, col_recv, row_own, row_recv, st_own, st_recv,
    part, ring_recv, second, second_recv, fg_recv,
    local_sem, gather_send, gather_recv, col_send, col_got, row_send, row_got, st_send, st_got,
    ring_send, ring_got, second_send, second_got, fg_send, fg_got,
):
    ny, nz, nf = geo
    local = tf.shape[0]
    bot = tv.shape[0]
    kl = tv.shape[1]
    rows = local * nf
    cb = kl // BLOCKS
    crops = rows * ny * nz
    protos = kl * nf
    dp, f = lax.axis_index("dp"), lax.axis_index("fsdp")
    y, z = dp // nz, lax.rem(dp, nz)

    def on_y(j):
        return {"dp": lax.rem(y + j, ny) * nz + z}

    def on_z(j):
        return {"dp": y * nz + lax.rem(z + j, nz)}

    def on_f(j):
        return {"fsdp": lax.rem(f + j, nf)}

    axes = ((on_y, ny, y), (on_z, nz, z))

    def block(j):
        return slice(j * cb, (j + 1) * cb)

    def send(src, dst, send_sem, recv_sem, device):
        pltpu.make_async_remote_copy(
            src_ref=src, dst_ref=dst, send_sem=send_sem, recv_sem=recv_sem,
            device_id=device, device_id_type=MESH,
        ).start()

    def took(ref, sem):
        pltpu.make_async_copy(ref, ref, sem).wait()

    loads = [
        pltpu.make_async_copy(src, dst, local_sem.at[i])
        for i, (src, dst) in enumerate(((tf_hbm, tf), (sf_hbm, sf), (tv_hbm, tv), (sv_hbm, sv)))
    ]
    for load in loads:
        load.start()
    barrier = pltpu.get_barrier_semaphore()
    for axis, n in ((on_f, nf), (on_y, ny), (on_z, nz)):
        for j in far_first(n):
            pl.semaphore_signal(barrier, inc=1, device_id=axis(j), device_id_type=MESH)

    own = pl.ds(pl.multiple_of(f * local, local), local)

    def unit_rows(ref):
        values = ref[...].astype(F32)
        length = jnp.sqrt(jnp.sum(values * values, axis=1, keepdims=True) + epsilon)
        return values / length, length

    loads[0].wait()
    tu[own, :] = unit_rows(tf)[0].astype(BF16)
    loads[1].wait()
    su[own, :] = unit_rows(sf)[0].astype(BF16)
    pl.semaphore_wait(barrier, nf + ny + nz - 3)

    def gather(i, unit):
        for j in far_first(nf):
            send(unit.at[own], unit.at[own], gather_send.at[i], gather_recv.at[i], on_f(j))

    gather(0, tu)
    others = pl.ds(0, rows - local)

    loads[2].wait()
    for j in range(BLOCKS):
        values = tv[:, block(j)].astype(F32)
        inverse = 1.0 / jnp.sqrt(jnp.sum(values * values, axis=0, keepdims=True) + epsilon)
        tv[:, block(j)] = (values * inverse).astype(BF16)

    def student_prototypes():
        loads[3].wait()
        for j in range(BLOCKS):
            values = sv[:, block(j)].astype(F32)
            inverse = 1.0 / jnp.sqrt(jnp.sum(values * values, axis=0, keepdims=True) + epsilon)
            winv[j : j + 1, :] = inverse
            sw[:, block(j)] = (values * inverse).astype(BF16)

    def student_orders():
        each = bot // (ny * nz)
        p = lax.broadcasted_iota(jnp.int32, (bot, bot), 0)
        d = lax.broadcasted_iota(jnp.int32, (bot, bot), 1)
        pz, py, pi = p // (ny * each), lax.rem(p // each, ny), lax.rem(p, each)
        perm[...] = (d == (py * nz + pz) * each + pi).astype(F32).astype(BF16)
        took(su.at[others], gather_recv.at[1])
        units = su[...]
        sut[0] = dot_nt((d == p).astype(F32).astype(BF16), units).astype(BF16)
        sut[1] = dot_nt(perm[...], units).astype(BF16)
        for j in range(HALF, BLOCKS):
            sv[:, block(j)] = dot_nn(perm[...], sv[:, block(j)]).astype(BF16)

    def student_mass():
        total = jnp.zeros((rows, 128), F32)
        for j in range(BLOCKS):
            values = jnp.exp(dot_nn(su[...], sw[:, block(j)]) * (1.0 / student_temp))
            prob[j] = values
            for c in range(0, cb, 128):
                total = total + values[:, c : c + 128]
        st_own[0] = lanes_of(total)
        i = lax.broadcasted_iota(jnp.int32, (local, rows), 0)
        c = lax.broadcasted_iota(jnp.int32, (local, rows), 1)
        place = (c == f * local + i).astype(F32).astype(BF16)
        st_own[1] = dot_nn(cw_ref[...], place)
        for j in far_first(nf):
            send(st_own, st_recv.at[j - 1], st_send, st_got, on_f(j))

    def col_first(it, h):
        axis, n, _ = axes[h]
        for j in far_first(n):
            send(col_own.at[it, h, 0], col_recv.at[it, h, 0, j - 1], col_send.at[it, h, 0], col_got.at[it, h, 0], axis(j))

    def col_total(it, h, stage):
        n = axes[(h + stage) % 2][1]
        took(col_recv.at[it, h, stage], col_got.at[it, h, stage])
        total = col_own[it, h, stage]
        for j in range(n - 1):
            total = total + col_recv[it, h, stage, j]
        return total

    def col_second(it, h):
        col_own[it, h, 1] = col_total(it, h, 0)
        axis, n, _ = axes[1 - h]
        for j in far_first(n):
            send(col_own.at[it, h, 1], col_recv.at[it, h, 1, j - 1], col_send.at[it, h, 1], col_got.at[it, h, 1], axis(j))

    student_prototypes()
    took(tu.at[others], gather_recv.at[0])
    gather(1, su)
    for it in range(ITERS):
        for h in range(2):
            for k in range(HALF):
                j = h * HALF + k
                if it == 0:
                    values = jnp.exp(dot_nn(tu[...], tv[:, block(j)]) * (1.0 / teacher_temp))
                    mass[j] = values
                else:
                    values = mass[j] * rb[...]
                col_own[it, h, 0, k : k + 1, :] = jnp.sum(values, axis=0, keepdims=True)

            col_first(it, h)
        if it == 0:
            student_orders()
        for h in range(2):
            col_second(it, h)
        if it == 0:
            student_mass()
        total = jnp.zeros((rows, 128), F32)
        for h in range(2):
            svec[h * HALF : (h + 1) * HALF, :] = 1.0 / (col_total(it, h, 1) * protos)
            for j in range(h * HALF, (h + 1) * HALF):
                values = mass[j] * svec[j : j + 1, :]
                for c in range(0, cb, 128):
                    total = total + values[:, c : c + 128]
        row_own[it] = lanes_of(total)
        for j in far_first(nf):
            send(row_own.at[it], row_recv.at[it, j - 1], row_send.at[it], row_got.at[it], on_f(j))
        if it == ITERS - 1:
            took(st_recv, st_got)
            student_total, weights = st_own[0], st_own[1]
            for j in range(nf - 1):
                student_total = student_total + st_recv[j, 0]
                weights = weights + st_recv[j, 1]
            ab[...] = rows_of(weights / (student_total * student_temp), cb)
        took(row_recv.at[it], row_got.at[it])
        row_total = row_own[it]
        for j in range(nf - 1):
            row_total = row_total + row_recv[it, j]
        if it < ITERS - 1:
            rb[...] = rows_of(1.0 / (row_total * crops), cb)
        else:
            bb[...] = rows_of(weights / (row_total * student_temp), cb)

    fg[...] = jnp.zeros_like(fg)
    rings = [(h, q) for q in range(4) for h in range(2)]

    def chunk(h, c):
        size = bot // axes[h][1]
        return pl.ds(pl.multiple_of(c * size, size), size)

    def lengths(h, q):
        n = axes[h][1]
        return (n // 2, (n - 1) // 2) if q % 2 == 0 else ((n - 1) // 2, n // 2)

    def chain_slot(h, q, way, s):
        return s if way == 0 else lengths(h, q)[0] + s

    def chain_step(h, q, way, s):
        axis, n, me = axes[h]
        r = 4 * h + q
        left = lengths(h, q)[way] - s
        c = lax.rem(me + (left if way == 0 else n - left), n)
        if s > 0:
            before = chain_slot(h, q, way, s - 1)
            took(ring_recv.at[r, before], ring_got.at[r, before])
            part[r, chunk(h, c), :] = part[r, chunk(h, c), :] + ring_recv[r, before]
        now = chain_slot(h, q, way, s)
        send(part.at[r, chunk(h, c)], ring_recv.at[r, now], ring_send.at[r], ring_got.at[r, now], axis(1 if way == 0 else n - 1))

    def chain_steps(h, q, s):
        for way in (0, 1) if q % 2 == 0 else (1, 0):
            if s < lengths(h, q)[way]:
                chain_step(h, q, way, s)

    for h, q in rings:
        r = 4 * h + q
        for k in range(2):
            j = 2 * r + k
            g = (prob[j] * ab[...] - mass[j] * bb[...] * svec[j : j + 1, :]).astype(BF16)
            fg[...] += dot_nt(g, sw[:, block(j)])
            grad = dot_nn(sut[h], g)
            inverse = winv[j : j + 1, :]
            w = sv[:, block(j)].astype(F32) * inverse
            inner = jnp.sum(w * grad, axis=0, keepdims=True)
            part[r, :, k * cb : (k + 1) * cb] = ((grad - w * inner) * inverse).astype(BF16)
        chain_steps(h, q, 0)

    def rows_at(i):
        return pl.ds(pl.multiple_of(i * local, local), local)

    for j in far_first(nf):
        send(fg.at[rows_at(lax.rem(f + j, nf))], fg_recv.at[j - 1], fg_send, fg_got, on_f(j))
    for s in range(1, max(ny, nz) // 2):
        for h, q in rings:
            chain_steps(h, q, s)

    each = bot // (ny * nz)
    for h in range(2):
        _, n, me = axes[h]
        sums = []
        for q in range(4):
            r = 4 * h + q
            total = part[r, chunk(h, me), :].astype(F32)
            for way in range(2):
                if lengths(h, q)[way]:
                    last = chain_slot(h, q, way, lengths(h, q)[way] - 1)
                    took(ring_recv.at[r, last], ring_got.at[r, last])
                    total = total + ring_recv[r, last].astype(F32)
            sums.append(total)
        axis, n2, me2 = axes[1 - h]
        for c in range(n2):
            second[h, c] = jnp.concatenate([total[c * each : (c + 1) * each] for total in sums], axis=0).astype(BF16)
        for j in far_first(n2):
            send(second.at[h, lax.rem(me2 + j, n2)], second_recv.at[h, j - 1], second_send.at[h], second_got.at[h], axis(j))

    took(fg_recv, fg_got)
    grad = fg[rows_at(f), :]
    for j in range(nf - 1):
        grad = grad + fg_recv[j]
    hat, length = unit_rows(sf)
    gf_ref[...] = (grad - hat * jnp.sum(hat * grad, axis=1, keepdims=True)) / length

    for h in range(2):
        took(second_recv.at[h], second_got.at[h])
        _, n2, me2 = axes[1 - h]
        total = second[h, me2].astype(F32)
        for j in range(n2 - 1):
            total = total + second_recv[h, j].astype(F32)
        for q in range(4):
            first = h * HALF * cb + q * 2 * cb
            gv_ref[:, first : first + 2 * cb] = total[q * each : (q + 1) * each]

    for i, unit in enumerate((tu, su)):
        took(unit.at[others], gather_send.at[i])
    for it in range(ITERS):
        for h in range(2):
            for stage in range(2):
                took(col_recv.at[it, h, stage], col_send.at[it, h, stage])
        took(row_recv.at[it], row_send.at[it])
    took(st_recv, st_send)
    took(fg_recv, fg_send)
    for h in range(2):
        for r in range(4 * h, 4 * h + 4):
            took(ring_recv.at[r], ring_send.at[r])
        took(second_recv.at[h], second_send.at[h])


def step(geo, teacher_feat, student_feat, crop_weight, teacher_v, student_v):
    ny, nz, nf = geo
    local, bot = teacher_feat.shape
    kl = teacher_v.shape[1]
    rows, cb = local * nf, kl // BLOCKS
    each = bot // (ny * nz)
    any_space = pl.BlockSpec(memory_space=pl.ANY)
    vmem = pl.BlockSpec(memory_space=pltpu.VMEM)
    dma = pltpu.SemaphoreType.DMA
    return pl.pallas_call(
        functools.partial(kernel, geo),
        out_shape=(
            jax.ShapeDtypeStruct((each, kl), F32),
            jax.ShapeDtypeStruct((local, bot), F32),
        ),
        in_specs=[any_space, any_space, vmem, any_space, any_space],
        out_specs=(vmem, vmem),
        scratch_shapes=[
            pltpu.VMEM((local, bot), BF16),
            pltpu.VMEM((local, bot), BF16),
            pltpu.VMEM((bot, kl), BF16),
            pltpu.VMEM((bot, kl), BF16),
            pltpu.VMEM((bot, kl), BF16),
            pltpu.VMEM((rows, bot), BF16),
            pltpu.VMEM((rows, bot), BF16),
            pltpu.VMEM((2, bot, rows), BF16),
            pltpu.VMEM((bot, bot), BF16),
            pltpu.VMEM((BLOCKS, rows, cb), F32),
            pltpu.VMEM((BLOCKS, rows, cb), F32),
            pltpu.VMEM((BLOCKS, cb), F32),
            pltpu.VMEM((BLOCKS, cb), F32),
            pltpu.VMEM((rows, cb), F32),
            pltpu.VMEM((rows, cb), F32),
            pltpu.VMEM((rows, cb), F32),
            pltpu.VMEM((rows, bot), F32),
            pltpu.VMEM((ITERS, 2, 2, HALF, cb), F32),
            pltpu.VMEM((ITERS, 2, 2, ny - 1, HALF, cb), F32),
            pltpu.VMEM((ITERS, 1, rows), F32),
            pltpu.VMEM((ITERS, nf - 1, 1, rows), F32),
            pltpu.VMEM((2, 1, rows), F32),
            pltpu.VMEM((nf - 1, 2, 1, rows), F32),
            pltpu.VMEM((8, bot, 2 * cb), BF16),
            pltpu.VMEM((8, ny - 1, bot // ny, 2 * cb), BF16),
            pltpu.VMEM((2, ny, 4 * each, 2 * cb), BF16),
            pltpu.VMEM((2, ny - 1, 4 * each, 2 * cb), BF16),
            pltpu.VMEM((nf - 1, local, bot), F32),
            dma((4,)),
            dma((2,)), dma((2,)),
            dma((ITERS, 2, 2)), dma((ITERS, 2, 2)),
            dma((ITERS,)), dma((ITERS,)),
            dma, dma,
            dma((8,)), dma((8, ny - 1)),
            dma((2,)), dma((2,)),
            dma, dma,
        ],
        compiler_params=pltpu.CompilerParams(
            collective_id=0, has_side_effects=True, vmem_limit_bytes=62 * 1024 * 1024
        ),
    )(teacher_feat, student_feat, crop_weight.reshape(1, local), teacher_v, student_v)


def solution(mesh, planes=(8, 8)):
    geo = (*planes, mesh.shape["fsdp"])
    placed = (
        P(("dp", "fsdp"), None),
        P(("dp", "fsdp"), None),
        P(("dp", "fsdp")),
        P(None, "fsdp"),
        P(None, "fsdp"),
    )
    return jax.shard_map(
        functools.partial(step, geo),
        mesh=mesh,
        in_specs=placed,
        out_specs=(P("dp", "fsdp"), P(("dp", "fsdp"), None)),
        check_vma=False,
    )
```

```python
import functools

import jax
import jax.numpy as jnp
from jax import lax
from jax.experimental import pallas as pl
from jax.experimental.pallas import tpu as pltpu
from jax.sharding import PartitionSpec as P

K = 32768
ITERS = 3
BLOCKS = 16
HALF = BLOCKS // 2
PARTS = 4
WIDE = HALF // PARTS
SKIP_FROM = 0

teacher_temp = 0.04
student_temp = 0.1
epsilon = 1e-06
F32 = jnp.float32
BF16 = jnp.bfloat16
MESH = pl.DeviceIdType.MESH


def far_first(n):
    return sorted(range(1, n), key=lambda j: -min(j, n - j))


def lanes_of(partial):
    return jnp.sum(jnp.transpose(partial), axis=0, keepdims=True)


def rows_of(vector, width):
    return jnp.transpose(jnp.broadcast_to(vector, (width, vector.shape[1])))


def dot_nt(a, b):
    return lax.dot_general(a, b, (((1,), (1,)), ((), ())), preferred_element_type=F32)


def dot_nn(a, b):
    return jnp.dot(a, b, preferred_element_type=F32)


def kernel(
    geo,
    tf_hbm, sf_hbm, cw_hbm, tv_hbm, sv_hbm,
    gv_ref, gf_ref,
    tf, sf, cw, tv, sv, sw, tu, su, sut, perm, mass, prob, winv, svec, rb, ab, bb, fg,
    sums, col_own, col_recv, row_own, row_recv, st_own, st_recv,
    part, ring_recv, second, second_recv, fg_recv,
    local_sem, gather_send, gather_recv, col_sent, col_got, row_send, row_got, st_send, st_got,
    ring_send, ring_got, second_send, second_got, fg_send, fg_got,
):
    ny, nz, nf = geo
    local = tf.shape[0]
    bot = tv.shape[0]
    kl = tv.shape[1]
    rows = local * nf
    cb = kl // BLOCKS
    crops = rows * ny * nz
    protos = kl * nf
    dp, f = lax.axis_index("dp"), lax.axis_index("fsdp")
    y, z = dp // nz, lax.rem(dp, nz)

    def on_y(j):
        return {"dp": lax.rem(y + j, ny) * nz + z}

    def on_z(j):
        return {"dp": y * nz + lax.rem(z + j, nz)}

    def on_f(j):
        return {"fsdp": lax.rem(f + j, nf)}

    axes = ((on_y, ny, y), (on_z, nz, z))

    def block(j):
        return slice(j * cb, (j + 1) * cb)

    def send(src, dst, send_sem, recv_sem, device):
        pltpu.make_async_remote_copy(
            src_ref=src, dst_ref=dst, send_sem=send_sem, recv_sem=recv_sem,
            device_id=device, device_id_type=MESH,
        ).start()

    def took(ref, sem):
        pltpu.make_async_copy(ref, ref, sem).wait()

    loads = [
        pltpu.make_async_copy(src, dst, local_sem.at[i])
        for i, (src, dst) in enumerate(((tf_hbm, tf), (sf_hbm, sf), (tv_hbm, tv), (sv_hbm, sv), (cw_hbm, cw)))
    ]
    for load in loads:
        load.start()
    barrier = pltpu.get_barrier_semaphore()
    for axis, n in ((on_f, nf), (on_y, ny), (on_z, nz)):
        for j in far_first(n):
            pl.semaphore_signal(barrier, inc=1, device_id=axis(j), device_id_type=MESH)

    own = pl.ds(pl.multiple_of(f * local, local), local)

    def unit_rows(ref):
        values = ref[...].astype(F32)
        length = jnp.sqrt(jnp.sum(values * values, axis=1, keepdims=True) + epsilon)
        return values / length, length

    loads[0].wait()
    tu[own, :] = unit_rows(tf)[0].astype(BF16)
    loads[1].wait()
    su[own, :] = unit_rows(sf)[0].astype(BF16)
    pl.semaphore_wait(barrier, nf + ny + nz - 3)

    def gather(i, unit):
        for j in far_first(nf):
            send(unit.at[own], unit.at[own], gather_send.at[i], gather_recv.at[i], on_f(j))

    gather(0, tu)
    others = pl.ds(0, rows - local)

    loads[2].wait()
    for j in range(BLOCKS):
        values = tv[:, block(j)].astype(F32)
        inverse = 1.0 / jnp.sqrt(jnp.sum(values * values, axis=0, keepdims=True) + epsilon)
        tv[:, block(j)] = (values * inverse).astype(BF16)

    def student_prototypes():
        loads[3].wait()
        for j in range(BLOCKS):
            values = sv[:, block(j)].astype(F32)
            inverse = 1.0 / jnp.sqrt(jnp.sum(values * values, axis=0, keepdims=True) + epsilon)
            winv[j : j + 1, :] = inverse
            sw[:, block(j)] = (values * inverse).astype(BF16)

    def student_orders():
        each = bot // (ny * nz)
        p = lax.broadcasted_iota(jnp.int32, (bot, bot), 0)
        d = lax.broadcasted_iota(jnp.int32, (bot, bot), 1)
        pz, py, pi = p // (ny * each), lax.rem(p // each, ny), lax.rem(p, each)
        perm[...] = (d == (py * nz + pz) * each + pi).astype(F32).astype(BF16)
        took(su.at[others], gather_recv.at[1])
        units = su[...]
        sut[0] = dot_nt((d == p).astype(F32).astype(BF16), units).astype(BF16)
        sut[1] = dot_nt(perm[...], units).astype(BF16)
        for j in range(HALF, BLOCKS):
            sv[:, block(j)] = dot_nn(perm[...], sv[:, block(j)]).astype(BF16)

    def student_mass():
        total = jnp.zeros((rows, 128), F32)
        for j in range(BLOCKS):
            values = jnp.exp(dot_nn(su[...], sw[:, block(j)]) * (1.0 / student_temp))
            prob[j] = values
            for c in range(0, cb, 128):
                total = total + values[:, c : c + 128]
        st_own[0] = lanes_of(total)
        i = lax.broadcasted_iota(jnp.int32, (local, rows), 0)
        c = lax.broadcasted_iota(jnp.int32, (local, rows), 1)
        place = (c == f * local + i).astype(F32).astype(BF16)
        loads[4].wait()
        st_own[1] = dot_nn(cw[...], place)
        for j in far_first(nf):
            send(st_own, st_recv.at[j - 1], st_send, st_got, on_f(j))

    def col_send(it, stage, sums):
        col_own[it, stage] = sums.astype(BF16)
        axis, n, _ = axes[stage]
        for j in far_first(n):
            send(col_own.at[it, stage], col_recv.at[it, stage, j - 1], col_sent.at[it, stage], col_got.at[it, stage], axis(j))

    def col_total(it, stage):
        took(col_recv.at[it, stage], col_got.at[it, stage])
        total = col_own[it, stage].astype(F32)
        for j in range(axes[stage][1] - 1):
            total = total + col_recv[it, stage, j].astype(F32)
        return total

    student_prototypes()
    took(tu.at[others], gather_recv.at[0])
    gather(1, su)
    for it in range(ITERS):
        for j in range(BLOCKS):
            if it == 0:
                values = jnp.exp(dot_nn(tu[...], tv[:, block(j)]) * (1.0 / teacher_temp))
                mass[j] = values
            else:
                values = mass[j] * rb[...]
            sums[j : j + 1, :] = jnp.sum(values, axis=0, keepdims=True)
        col_send(it, 0, sums[...])
        if it == 0:
            student_orders()
        col_send(it, 1, col_total(it, 0))
        if it == 0:
            student_mass()
        svec[...] = 1.0 / (col_total(it, 1) * protos)
        total = jnp.zeros((rows, 128), F32)
        for j in range(BLOCKS):
            values = mass[j] * svec[j : j + 1, :]
            for c in range(0, cb, 128):
                total = total + values[:, c : c + 128]
        row_own[it] = lanes_of(total)
        for j in far_first(nf):
            send(row_own.at[it], row_recv.at[it, j - 1], row_send.at[it], row_got.at[it], on_f(j))
        if it == ITERS - 1:
            took(st_recv, st_got)
            student_total, weights = st_own[0], st_own[1]
            for j in range(nf - 1):
                student_total = student_total + st_recv[j, 0]
                weights = weights + st_recv[j, 1]
            ab[...] = rows_of(weights / (student_total * student_temp), cb)
        took(row_recv.at[it], row_got.at[it])
        row_total = row_own[it]
        for j in range(nf - 1):
            row_total = row_total + row_recv[it, j]
        if it < ITERS - 1:
            rb[...] = rows_of(1.0 / (row_total * crops), cb)
        else:
            bb[...] = rows_of(weights / (row_total * student_temp), cb)

    fg[...] = jnp.zeros_like(fg)
    rings = [(h, q) for q in range(PARTS) for h in range(2)]

    def chunk(h, c):
        size = bot // axes[h][1]
        return pl.ds(pl.multiple_of(c * size, size), size)

    def length(h, q, way):
        n = axes[h][1]
        return n // 2 if way == q % 2 else (n - 1) // 2

    def slot(h, q, way, far):
        return (length(h, q, 0) if way else 0) + far - 1

    def skips(h, q, way):
        return length(h, q, way) % 2 == 0 and q >= SKIP_FROM

    def senders(h, q, way, far):
        n = length(h, q, way)
        if skips(h, q, way) and far == n - 2:
            return (n, n - 1)
        if far == n or (skips(h, q, way) and far == n - 1):
            return ()
        return (far + 1,)

    def chain_step(h, q, way, far):
        axis, n, me = axes[h]
        r, last = PARTS * h + q, length(h, q, way)
        rows_to = chunk(h, lax.rem(me + (far if way == 0 else n - far), n))
        for sender in senders(h, q, way, far):
            got = slot(h, q, way, sender)
            took(ring_recv.at[r, got], ring_got.at[r, got])
            part[r, rows_to, :] = part[r, rows_to, :] + ring_recv[r, got]
        hops = 2 if skips(h, q, way) and far == last else 1
        now = slot(h, q, way, far)
        send(
            part.at[r, rows_to], ring_recv.at[r, now], ring_send.at[r], ring_got.at[r, now],
            axis(hops if way == 0 else n - hops),
        )

    def chain_steps(h, q, s):
        for way in (q % 2, 1 - q % 2):
            last = length(h, q, way)
            for far in range(last, 0, -1):
                at = max(last - far - 1, 0) if skips(h, q, way) else last - far
                if at == s:
                    chain_step(h, q, way, far)

    for h, q in rings:
        r = PARTS * h + q
        for k in range(WIDE):
            j = WIDE * r + k
            g = (prob[j] * ab[...] - mass[j] * bb[...] * svec[j : j + 1, :]).astype(BF16)
            fg[...] += dot_nt(g, sw[:, block(j)])
            grad = dot_nn(sut[h], g)
            inverse = winv[j : j + 1, :]
            w = sv[:, block(j)].astype(F32) * inverse
            inner = jnp.sum(w * grad, axis=0, keepdims=True)
            part[r, :, k * cb : (k + 1) * cb] = ((grad - w * inner) * inverse).astype(BF16)
        chain_steps(h, q, 0)

    def rows_at(i):
        return pl.ds(pl.multiple_of(i * local, local), local)

    for j in far_first(nf):
        send(fg.at[rows_at(lax.rem(f + j, nf))], fg_recv.at[j - 1], fg_send, fg_got, on_f(j))
    for s in range(1, max(ny, nz) // 2):
        for h, q in rings:
            chain_steps(h, q, s)

    each = bot // (ny * nz)
    for h in range(2):
        _, n, me = axes[h]
        totals = []
        for q in range(PARTS):
            r = PARTS * h + q
            total = part[r, chunk(h, me), :].astype(F32)
            for way in range(2):
                for sender in senders(h, q, way, 0):
                    got = slot(h, q, way, sender)
                    took(ring_recv.at[r, got], ring_got.at[r, got])
                    total = total + ring_recv[r, got].astype(F32)
            totals.append(total)
        totals = jnp.concatenate(totals, axis=1)
        totals = [totals[:, k * cb : (k + 2) * cb] for k in range(0, HALF, 2)]
        axis, n2, me2 = axes[1 - h]
        for c in range(n2):
            second[h, c] = jnp.concatenate([total[c * each : (c + 1) * each] for total in totals], axis=0).astype(BF16)
        for j in far_first(n2):
            send(second.at[h, lax.rem(me2 + j, n2)], second_recv.at[h, j - 1], second_send.at[h], second_got.at[h], axis(j))

    took(fg_recv, fg_got)
    grad = fg[rows_at(f), :]
    for j in range(nf - 1):
        grad = grad + fg_recv[j]
    hat, length = unit_rows(sf)
    gf_ref[...] = (grad - hat * jnp.sum(hat * grad, axis=1, keepdims=True)) / length

    for h in range(2):
        took(second_recv.at[h], second_got.at[h])
        _, n2, me2 = axes[1 - h]
        total = second[h, me2].astype(F32)
        for j in range(n2 - 1):
            total = total + second_recv[h, j].astype(F32)
        for q in range(4):
            first = h * HALF * cb + q * 2 * cb
            gv_ref[:, first : first + 2 * cb] = total[q * each : (q + 1) * each]

    for i, unit in enumerate((tu, su)):
        took(unit.at[others], gather_send.at[i])
    for it in range(ITERS):
        for stage in range(2):
            took(col_recv.at[it, stage], col_sent.at[it, stage])
        took(row_recv.at[it], row_send.at[it])
    took(st_recv, st_send)
    took(fg_recv, fg_send)
    for h in range(2):
        for r in range(PARTS * h, PARTS * (h + 1)):
            took(ring_recv.at[r], ring_send.at[r])
        took(second_recv.at[h], second_send.at[h])


def hand_over(gv_ref, gf_ref, gv_out, gf_out):
    gv_out[...] = gv_ref[...]
    gf_out[...] = gf_ref[...]


def step(geo, teacher_feat, student_feat, crop_weight, teacher_v, student_v):
    ny, nz, nf = geo
    local, bot = teacher_feat.shape
    kl = teacher_v.shape[1]
    rows, cb = local * nf, kl // BLOCKS
    each = bot // (ny * nz)
    any_space = pl.BlockSpec(memory_space=pl.ANY)
    vmem = pl.BlockSpec(memory_space=pltpu.VMEM)
    dma = pltpu.SemaphoreType.DMA
    grads = pl.pallas_call(
        functools.partial(kernel, geo),
        out_shape=(
            jax.ShapeDtypeStruct((each, kl), F32),
            jax.ShapeDtypeStruct((local, bot), F32),
        ),
        in_specs=[any_space] * 5,
        out_specs=(vmem, vmem),
        scratch_shapes=[
            pltpu.VMEM((local, bot), BF16),
            pltpu.VMEM((local, bot), BF16),
            pltpu.VMEM((1, local), BF16),
            pltpu.VMEM((bot, kl), BF16),
            pltpu.VMEM((bot, kl), BF16),
            pltpu.VMEM((bot, kl), BF16),
            pltpu.VMEM((rows, bot), BF16),
            pltpu.VMEM((rows, bot), BF16),
            pltpu.VMEM((2, bot, rows), BF16),
            pltpu.VMEM((bot, bot), BF16),
            pltpu.VMEM((BLOCKS, rows, cb), F32),
            pltpu.VMEM((BLOCKS, rows, cb), F32),
            pltpu.VMEM((BLOCKS, cb), F32),
            pltpu.VMEM((BLOCKS, cb), F32),
            pltpu.VMEM((rows, cb), F32),
            pltpu.VMEM((rows, cb), F32),
            pltpu.VMEM((rows, cb), F32),
            pltpu.VMEM((rows, bot), F32),
            pltpu.VMEM((BLOCKS, cb), F32),
            pltpu.VMEM((ITERS, 2, BLOCKS, cb), BF16),
            pltpu.VMEM((ITERS, 2, ny - 1, BLOCKS, cb), BF16),
            pltpu.VMEM((ITERS, 1, rows), F32),
            pltpu.VMEM((ITERS, nf - 1, 1, rows), F32),
            pltpu.VMEM((2, 1, rows), F32),
            pltpu.VMEM((nf - 1, 2, 1, rows), F32),
            pltpu.VMEM((2 * PARTS, bot, WIDE * cb), BF16),
            pltpu.VMEM((2 * PARTS, ny - 1, bot // ny, WIDE * cb), BF16),
            pltpu.VMEM((2, ny, 4 * each, 2 * cb), BF16),
            pltpu.VMEM((2, ny - 1, 4 * each, 2 * cb), BF16),
            pltpu.VMEM((nf - 1, local, bot), F32),
            dma((5,)),
            dma((2,)), dma((2,)),
            dma((ITERS, 2)), dma((ITERS, 2)),
            dma((ITERS,)), dma((ITERS,)),
            dma, dma,
            dma((2 * PARTS,)), dma((2 * PARTS, ny - 1)),
            dma((2,)), dma((2,)),
            dma, dma,
        ],
        compiler_params=pltpu.CompilerParams(
            collective_id=0, has_side_effects=True, vmem_limit_bytes=62 * 1024 * 1024
        ),
    )(teacher_feat, student_feat, crop_weight.reshape(1, local), teacher_v, student_v)
    return pl.pallas_call(
        hand_over,
        out_shape=[jax.ShapeDtypeStruct(grad.shape, grad.dtype) for grad in grads],
        in_specs=[vmem, vmem],
        out_specs=[vmem, vmem],
    )(*grads)


def solution(mesh, planes=(8, 8)):
    geo = (*planes, mesh.shape["fsdp"])
    placed = (
        P(("dp", "fsdp"), None),
        P(("dp", "fsdp"), None),
        P(("dp", "fsdp")),
        P(None, "fsdp"),
        P(None, "fsdp"),
    )
    return jax.shard_map(
        functools.partial(step, geo),
        mesh=mesh,
        in_specs=placed,
        out_specs=(P("dp", "fsdp"), P(("dp", "fsdp"), None)),
        check_vma=False,
    )
```

```python
import functools

import jax
import jax.numpy as jnp
from jax import lax
from jax.experimental import pallas as pl
from jax.experimental.pallas import tpu as pltpu
from jax.sharding import PartitionSpec as P

K = 32768
ITERS = 3
BLOCKS = 16
HALF = BLOCKS // 2
PARTS = 4
WIDE = HALF // PARTS
ROUTES = (1, 1, 1, 2)
TOWARDS = {
    0: ((), (), ()),
    1: ((0,), (0,), (0,)),
    2: ((0, 1), (0, 0), (0, 0)),
    3: ((0, 1, 2), (0, 1, 2), (0, 0, 2)),
    4: ((0, 1, 2, 3), (0, 1, 2, 2), (0, 0, 2, 2)),
}

teacher_temp = 0.04
student_temp = 0.1
epsilon = 1e-06
F32 = jnp.float32
BF16 = jnp.bfloat16
MESH = pl.DeviceIdType.MESH


def far_first(n):
    return sorted(range(1, n), key=lambda j: -min(j, n - j))


def lanes_of(partial):
    return jnp.sum(jnp.transpose(partial), axis=0, keepdims=True)


def rows_of(vector, width):
    return jnp.transpose(jnp.broadcast_to(vector, (width, vector.shape[1])))


def dot_nt(a, b):
    return lax.dot_general(a, b, (((1,), (1,)), ((), ())), preferred_element_type=F32)


def dot_nn(a, b):
    return jnp.dot(a, b, preferred_element_type=F32)


def kernel(
    geo,
    tf_hbm, sf_hbm, cw_hbm, tv_hbm, sv_hbm,
    gv_ref, gf_ref,
    tf, sf, cw, tv, sv, sw, tu, su, sut, perm, mass, prob, winv, svec, rb, ab, bb, fg,
    sums, col_own, col_recv, row_own, row_recv, st_own, st_recv,
    part, ring_recv, second, second_recv, fg_recv,
    told, local_sem, gather_send, gather_recv, col_sent, col_got, row_send, row_got, st_send, st_got,
    ring_send, ring_got, second_send, second_got, fg_send, fg_got,
):
    ny, nz, nf = geo
    local = tf.shape[0]
    bot = tv.shape[0]
    kl = tv.shape[1]
    rows = local * nf
    cb = kl // BLOCKS
    crops = rows * ny * nz
    protos = kl * nf
    dp, f = lax.axis_index("dp"), lax.axis_index("fsdp")
    y, z = dp // nz, lax.rem(dp, nz)

    def on_y(j):
        return {"dp": lax.rem(y + j, ny) * nz + z}

    def on_z(j):
        return {"dp": y * nz + lax.rem(z + j, nz)}

    def on_f(j):
        return {"fsdp": lax.rem(f + j, nf)}

    axes = ((on_y, ny, y), (on_z, nz, z))

    def block(j):
        return slice(j * cb, (j + 1) * cb)

    def send(src, dst, send_sem, recv_sem, device):
        pltpu.make_async_remote_copy(
            src_ref=src, dst_ref=dst, send_sem=send_sem, recv_sem=recv_sem,
            device_id=device, device_id_type=MESH,
        ).start()

    def took(ref, sem):
        pltpu.make_async_copy(ref, ref, sem).wait()

    loads = [
        pltpu.make_async_copy(src, dst, local_sem.at[i])
        for i, (src, dst) in enumerate(((tf_hbm, tf), (sf_hbm, sf), (tv_hbm, tv), (sv_hbm, sv), (cw_hbm, cw)))
    ]
    for load in loads:
        load.start()
    barrier = pltpu.get_barrier_semaphore()
    greeted = [on_f(j) for j in far_first(nf)]
    for axis, n, _ in axes:
        greeted += [axis(j) for j in sorted({1, n - 1})]
    for device in greeted:
        pl.semaphore_signal(barrier, inc=1, device_id=device, device_id_type=MESH)

    own = pl.ds(pl.multiple_of(f * local, local), local)

    def unit_rows(ref):
        values = ref[...].astype(F32)
        length = jnp.sqrt(jnp.sum(values * values, axis=1, keepdims=True) + epsilon)
        return values / length, length

    loads[0].wait()
    tu[own, :] = unit_rows(tf)[0].astype(BF16)
    loads[1].wait()
    su[own, :] = unit_rows(sf)[0].astype(BF16)
    pl.semaphore_wait(barrier, len(greeted))

    def tell(reach):
        for a, (axis, n, _) in enumerate(axes):
            for j in (reach, n - reach) if 2 * reach < n else ():
                pl.semaphore_signal(told.at[a, reach // 2], inc=1, device_id=axis(j), device_id_type=MESH)

    def hear(reach):
        for a, (_, n, _) in enumerate(axes):
            if 2 * reach < n:
                pl.semaphore_wait(told.at[a, reach // 2], 2)

    def gather(i, unit):
        for j in far_first(nf):
            send(unit.at[own], unit.at[own], gather_send.at[i], gather_recv.at[i], on_f(j))

    gather(0, tu)
    tell(1)
    others = pl.ds(0, rows - local)

    loads[2].wait()
    for j in range(BLOCKS):
        values = tv[:, block(j)].astype(F32)
        inverse = 1.0 / jnp.sqrt(jnp.sum(values * values, axis=0, keepdims=True) + epsilon)
        tv[:, block(j)] = (values * inverse).astype(BF16)
    hear(1)
    tell(2)

    def student_prototypes():
        loads[3].wait()
        for j in range(BLOCKS):
            values = sv[:, block(j)].astype(F32)
            inverse = 1.0 / jnp.sqrt(jnp.sum(values * values, axis=0, keepdims=True) + epsilon)
            winv[j : j + 1, :] = inverse
            sw[:, block(j)] = (values * inverse).astype(BF16)

    def student_orders():
        each = bot // (ny * nz)
        p = lax.broadcasted_iota(jnp.int32, (bot, bot), 0)
        d = lax.broadcasted_iota(jnp.int32, (bot, bot), 1)
        pz, py, pi = p // (ny * each), lax.rem(p // each, ny), lax.rem(p, each)
        perm[...] = (d == (py * nz + pz) * each + pi).astype(F32).astype(BF16)
        took(su.at[others], gather_recv.at[1])
        units = su[...]
        sut[0] = dot_nt((d == p).astype(F32).astype(BF16), units).astype(BF16)
        sut[1] = dot_nt(perm[...], units).astype(BF16)
        for j in range(HALF, BLOCKS):
            sv[:, block(j)] = dot_nn(perm[...], sv[:, block(j)]).astype(BF16)

    def student_mass():
        total = jnp.zeros((rows, 128), F32)
        for j in range(BLOCKS):
            values = jnp.exp(dot_nn(su[...], sw[:, block(j)]) * (1.0 / student_temp))
            prob[j] = values
            for c in range(0, cb, 128):
                total = total + values[:, c : c + 128]
        st_own[0] = lanes_of(total)
        i = lax.broadcasted_iota(jnp.int32, (local, rows), 0)
        c = lax.broadcasted_iota(jnp.int32, (local, rows), 1)
        place = (c == f * local + i).astype(F32).astype(BF16)
        loads[4].wait()
        st_own[1] = dot_nn(cw[...], place)
        for j in far_first(nf):
            send(st_own, st_recv.at[j - 1], st_send, st_got, on_f(j))

    def col_send(it, stage, sums):
        col_own[it, stage] = sums.astype(BF16)
        axis, n, _ = axes[stage]
        for j in far_first(n):
            send(col_own.at[it, stage], col_recv.at[it, stage, j - 1], col_sent.at[it, stage], col_got.at[it, stage], axis(j))

    def col_total(it, stage):
        took(col_recv.at[it, stage], col_got.at[it, stage])
        total = col_own[it, stage].astype(F32)
        for j in range(axes[stage][1] - 1):
            total = total + col_recv[it, stage, j].astype(F32)
        return total

    student_prototypes()
    hear(2)
    took(tu.at[others], gather_recv.at[0])
    gather(1, su)
    for it in range(ITERS):
        for j in range(BLOCKS):
            if it == 0:
                values = jnp.exp(dot_nn(tu[...], tv[:, block(j)]) * (1.0 / teacher_temp))
                mass[j] = values
            else:
                values = mass[j] * rb[...]
            sums[j : j + 1, :] = jnp.sum(values, axis=0, keepdims=True)
        col_send(it, 0, sums[...])
        if it == 0:
            student_orders()
        col_send(it, 1, col_total(it, 0))
        if it == 0:
            student_mass()
        svec[...] = 1.0 / (col_total(it, 1) * protos)
        total = jnp.zeros((rows, 128), F32)
        for j in range(BLOCKS):
            values = mass[j] * svec[j : j + 1, :]
            for c in range(0, cb, 128):
                total = total + values[:, c : c + 128]
        row_own[it] = lanes_of(total)
        for j in far_first(nf):
            send(row_own.at[it], row_recv.at[it, j - 1], row_send.at[it], row_got.at[it], on_f(j))
        if it == ITERS - 1:
            took(st_recv, st_got)
            student_total, weights = st_own[0], st_own[1]
            for j in range(nf - 1):
                student_total = student_total + st_recv[j, 0]
                weights = weights + st_recv[j, 1]
            ab[...] = rows_of(weights / (student_total * student_temp), cb)
        took(row_recv.at[it], row_got.at[it])
        row_total = row_own[it]
        for j in range(nf - 1):
            row_total = row_total + row_recv[it, j]
        if it < ITERS - 1:
            rb[...] = rows_of(1.0 / (row_total * crops), cb)
        else:
            bb[...] = rows_of(weights / (row_total * student_temp), cb)

    fg[...] = jnp.zeros_like(fg)
    rings = [(h, q) for q in range(PARTS) for h in range(2)]

    def chunk(h, c):
        size = bot // axes[h][1]
        return pl.ds(pl.multiple_of(c * size, size), size)

    def length(h, q, way):
        n = axes[h][1]
        return n // 2 if way == q % 2 else (n - 1) // 2

    def slot(h, q, way, far):
        return (length(h, q, 0) if way else 0) + far - 1

    def towards(h, q, way, far):
        return TOWARDS[length(h, q, way)][ROUTES[q]][far - 1]

    def senders(h, q, way, far):
        return [other for other in range(length(h, q, way), far, -1) if towards(h, q, way, other) == far]

    def depth(h, q, way, far):
        return 0 if far == 0 else 1 + depth(h, q, way, towards(h, q, way, far))

    def chain_step(h, q, way, far):
        axis, n, me = axes[h]
        r = PARTS * h + q
        rows_to = chunk(h, lax.rem(me + (far if way == 0 else n - far), n))
        for sender in senders(h, q, way, far):
            got = slot(h, q, way, sender)
            took(ring_recv.at[r, got], ring_got.at[r, got])
            part[r, rows_to, :] = part[r, rows_to, :] + ring_recv[r, got]
        hops = far - towards(h, q, way, far)
        now = slot(h, q, way, far)
        send(
            part.at[r, rows_to], ring_recv.at[r, now], ring_send.at[r], ring_got.at[r, now],
            axis(hops if way == 0 else n - hops),
        )

    def chain_steps(h, q, s):
        for way in (q % 2, 1 - q % 2):
            far_ones = range(length(h, q, way), 0, -1)
            steps = max([depth(h, q, way, far) for far in far_ones], default=0)
            for far in far_ones:
                if steps - depth(h, q, way, far) == s:
                    chain_step(h, q, way, far)

    for h, q in rings:
        r = PARTS * h + q
        for k in range(WIDE):
            j = WIDE * r + k
            g = (prob[j] * ab[...] - mass[j] * bb[...] * svec[j : j + 1, :]).astype(BF16)
            fg[...] += dot_nt(g, sw[:, block(j)])
            grad = dot_nn(sut[h], g)
            inverse = winv[j : j + 1, :]
            w = sv[:, block(j)].astype(F32) * inverse
            inner = jnp.sum(w * grad, axis=0, keepdims=True)
            part[r, :, k * cb : (k + 1) * cb] = ((grad - w * inner) * inverse).astype(BF16)
        chain_steps(h, q, 0)

    def rows_at(i):
        return pl.ds(pl.multiple_of(i * local, local), local)

    for j in far_first(nf):
        send(fg.at[rows_at(lax.rem(f + j, nf))], fg_recv.at[j - 1], fg_send, fg_got, on_f(j))
    for s in range(1, max(ny, nz) // 2):
        for h, q in rings:
            chain_steps(h, q, s)

    each = bot // (ny * nz)
    for h in range(2):
        _, n, me = axes[h]
        totals = []
        for q in range(PARTS):
            r = PARTS * h + q
            total = part[r, chunk(h, me), :].astype(F32)
            for way in range(2):
                for sender in senders(h, q, way, 0):
                    got = slot(h, q, way, sender)
                    took(ring_recv.at[r, got], ring_got.at[r, got])
                    total = total + ring_recv[r, got].astype(F32)
            totals.append(total)
        totals = jnp.concatenate(totals, axis=1)
        totals = [totals[:, k * cb : (k + 2) * cb] for k in range(0, HALF, 2)]
        axis, n2, me2 = axes[1 - h]
        for c in range(n2):
            second[h, c] = jnp.concatenate([total[c * each : (c + 1) * each] for total in totals], axis=0).astype(BF16)
        for j in far_first(n2):
            send(second.at[h, lax.rem(me2 + j, n2)], second_recv.at[h, j - 1], second_send.at[h], second_got.at[h], axis(j))

    took(fg_recv, fg_got)
    grad = fg[rows_at(f), :]
    for j in range(nf - 1):
        grad = grad + fg_recv[j]
    hat, length = unit_rows(sf)
    gf_ref[...] = (grad - hat * jnp.sum(hat * grad, axis=1, keepdims=True)) / length

    for h in range(2):
        took(second_recv.at[h], second_got.at[h])
        _, n2, me2 = axes[1 - h]
        total = second[h, me2].astype(F32)
        for j in range(n2 - 1):
            total = total + second_recv[h, j].astype(F32)
        for q in range(4):
            first = h * HALF * cb + q * 2 * cb
            gv_ref[:, first : first + 2 * cb] = total[q * each : (q + 1) * each]

    for i, unit in enumerate((tu, su)):
        took(unit.at[others], gather_send.at[i])
    for it in range(ITERS):
        for stage in range(2):
            took(col_recv.at[it, stage], col_sent.at[it, stage])
        took(row_recv.at[it], row_send.at[it])
    took(st_recv, st_send)
    took(fg_recv, fg_send)
    for h in range(2):
        for r in range(PARTS * h, PARTS * (h + 1)):
            took(ring_recv.at[r], ring_send.at[r])
        took(second_recv.at[h], second_send.at[h])


def hand_over(gv_ref, gf_ref, gv_out, gf_out):
    gv_out[...] = gv_ref[...]
    gf_out[...] = gf_ref[...]


def step(geo, teacher_feat, student_feat, crop_weight, teacher_v, student_v):
    ny, nz, nf = geo
    local, bot = teacher_feat.shape
    kl = teacher_v.shape[1]
    rows, cb = local * nf, kl // BLOCKS
    each = bot // (ny * nz)
    any_space = pl.BlockSpec(memory_space=pl.ANY)
    vmem = pl.BlockSpec(memory_space=pltpu.VMEM)
    dma = pltpu.SemaphoreType.DMA
    grads = pl.pallas_call(
        functools.partial(kernel, geo),
        out_shape=(
            jax.ShapeDtypeStruct((each, kl), F32),
            jax.ShapeDtypeStruct((local, bot), F32),
        ),
        in_specs=[any_space] * 5,
        out_specs=(vmem, vmem),
        scratch_shapes=[
            pltpu.VMEM((local, bot), BF16),
            pltpu.VMEM((local, bot), BF16),
            pltpu.VMEM((1, local), BF16),
            pltpu.VMEM((bot, kl), BF16),
            pltpu.VMEM((bot, kl), BF16),
            pltpu.VMEM((bot, kl), BF16),
            pltpu.VMEM((rows, bot), BF16),
            pltpu.VMEM((rows, bot), BF16),
            pltpu.VMEM((2, bot, rows), BF16),
            pltpu.VMEM((bot, bot), BF16),
            pltpu.VMEM((BLOCKS, rows, cb), F32),
            pltpu.VMEM((BLOCKS, rows, cb), F32),
            pltpu.VMEM((BLOCKS, cb), F32),
            pltpu.VMEM((BLOCKS, cb), F32),
            pltpu.VMEM((rows, cb), F32),
            pltpu.VMEM((rows, cb), F32),
            pltpu.VMEM((rows, cb), F32),
            pltpu.VMEM((rows, bot), F32),
            pltpu.VMEM((BLOCKS, cb), F32),
            pltpu.VMEM((ITERS, 2, BLOCKS, cb), BF16),
            pltpu.VMEM((ITERS, 2, ny - 1, BLOCKS, cb), BF16),
            pltpu.VMEM((ITERS, 1, rows), F32),
            pltpu.VMEM((ITERS, nf - 1, 1, rows), F32),
            pltpu.VMEM((2, 1, rows), F32),
            pltpu.VMEM((nf - 1, 2, 1, rows), F32),
            pltpu.VMEM((2 * PARTS, bot, WIDE * cb), BF16),
            pltpu.VMEM((2 * PARTS, ny - 1, bot // ny, WIDE * cb), BF16),
            pltpu.VMEM((2, ny, 4 * each, 2 * cb), BF16),
            pltpu.VMEM((2, ny - 1, 4 * each, 2 * cb), BF16),
            pltpu.VMEM((nf - 1, local, bot), F32),
            pltpu.SemaphoreType.REGULAR((2, 2)),
            dma((5,)),
            dma((2,)), dma((2,)),
            dma((ITERS, 2)), dma((ITERS, 2)),
            dma((ITERS,)), dma((ITERS,)),
            dma, dma,
            dma((2 * PARTS,)), dma((2 * PARTS, ny - 1)),
            dma((2,)), dma((2,)),
            dma, dma,
        ],
        compiler_params=pltpu.CompilerParams(
            collective_id=0, has_side_effects=True, vmem_limit_bytes=62 * 1024 * 1024
        ),
    )(teacher_feat, student_feat, crop_weight.reshape(1, local), teacher_v, student_v)
    return pl.pallas_call(
        hand_over,
        out_shape=[jax.ShapeDtypeStruct(grad.shape, grad.dtype) for grad in grads],
        in_specs=[vmem, vmem],
        out_specs=[vmem, vmem],
    )(*grads)


def solution(mesh, planes=(8, 8)):
    geo = (*planes, mesh.shape["fsdp"])
    placed = (
        P(("dp", "fsdp"), None),
        P(("dp", "fsdp"), None),
        P(("dp", "fsdp")),
        P(None, "fsdp"),
        P(None, "fsdp"),
    )
    return jax.shard_map(
        functools.partial(step, geo),
        mesh=mesh,
        in_specs=placed,
        out_specs=(P("dp", "fsdp"), P(("dp", "fsdp"), None)),
        check_vma=False,
    )
```

```python
import functools

import jax
import jax.numpy as jnp
from jax import lax
from jax.experimental import pallas as pl
from jax.experimental.pallas import tpu as pltpu
from jax.sharding import PartitionSpec as P

K = 32768
ITERS = 3
BLOCKS = 16
HALF = BLOCKS // 2
PARTS = 4
WIDE = HALF // PARTS
ROUTES = (1, 1, 1, 2)
TOWARDS = {
    0: ((), (), ()),
    1: ((0,), (0,), (0,)),
    2: ((0, 1), (0, 0), (0, 0)),
    3: ((0, 1, 2), (0, 1, 2), (0, 0, 2)),
    4: ((0, 1, 2, 3), (0, 1, 2, 2), (0, 0, 2, 2)),
}

teacher_temp = 0.04
student_temp = 0.1
epsilon = 1e-06
F32 = jnp.float32
BF16 = jnp.bfloat16
MESH = pl.DeviceIdType.MESH


def far_first(n):
    return sorted(range(1, n), key=lambda j: -min(j, n - j))


def lanes_of(partial):
    return jnp.sum(jnp.transpose(partial), axis=0, keepdims=True)


def rows_of(vector, width):
    return jnp.transpose(jnp.broadcast_to(vector, (width, vector.shape[1])))


def dot_nt(a, b):
    return lax.dot_general(a, b, (((1,), (1,)), ((), ())), preferred_element_type=F32)


def dot_nn(a, b):
    return jnp.dot(a, b, preferred_element_type=F32)


def kernel(
    geo,
    tf_hbm, sf_hbm, cw_hbm, tv_hbm, sv_hbm,
    gv_ref, gf_ref,
    tf, sf, cw, tv, sv, sw, tu, su, sut, perm, mass, prob, winv, svec, rb, ab, bb, fg,
    sums, col_own, col_recv, row_own, row_recv, st_own, st_recv,
    part, ring_recv, second, second_recv, fg_recv,
    told, local_sem, gather_send, gather_recv, col_sent, col_got, row_send, row_got, st_send, st_got,
    ring_send, ring_got, second_send, second_got, fg_send, fg_got,
):
    ny, nz, nf = geo
    local = tf.shape[0]
    bot = tv.shape[0]
    kl = tv.shape[1]
    rows = local * nf
    cb = kl // BLOCKS
    crops = rows * ny * nz
    protos = kl * nf
    dp, f = lax.axis_index("dp"), lax.axis_index("fsdp")
    y, z = dp // nz, lax.rem(dp, nz)

    def on_y(j):
        return {"dp": lax.rem(y + j, ny) * nz + z}

    def on_z(j):
        return {"dp": y * nz + lax.rem(z + j, nz)}

    def on_f(j):
        return {"fsdp": lax.rem(f + j, nf)}

    axes = ((on_y, ny, y), (on_z, nz, z))

    def block(j):
        return slice(j * cb, (j + 1) * cb)

    def send(src, dst, send_sem, recv_sem, device):
        pltpu.make_async_remote_copy(
            src_ref=src, dst_ref=dst, send_sem=send_sem, recv_sem=recv_sem,
            device_id=device, device_id_type=MESH,
        ).start()

    def took(ref, sem):
        pltpu.make_async_copy(ref, ref, sem).wait()

    loads = [
        pltpu.make_async_copy(src, dst, local_sem.at[i])
        for i, (src, dst) in enumerate(((tf_hbm, tf), (sf_hbm, sf), (tv_hbm, tv), (sv_hbm, sv), (cw_hbm, cw)))
    ]
    barrier = pltpu.get_barrier_semaphore()
    greeted = [on_f(j) for j in far_first(nf)]
    for axis, n, _ in axes:
        greeted += [axis(j) for j in sorted({1, n - 1})]
    for device in greeted:
        pl.semaphore_signal(barrier, inc=1, device_id=device, device_id_type=MESH)
    for i in (0, 2, 1, 4, 3):
        loads[i].start()

    own = pl.ds(pl.multiple_of(f * local, local), local)

    def unit_rows(ref):
        values = ref[...].astype(F32)
        length = jnp.sqrt(jnp.sum(values * values, axis=1, keepdims=True) + epsilon)
        return values / length, length

    loads[0].wait()
    tu[own, :] = unit_rows(tf)[0].astype(BF16)
    pl.semaphore_wait(barrier, len(greeted))

    def tell(reach):
        for a, (axis, n, _) in enumerate(axes):
            for j in (reach, n - reach) if 2 * reach < n else ():
                pl.semaphore_signal(told.at[a, reach // 2], inc=1, device_id=axis(j), device_id_type=MESH)

    def hear(reach):
        for a, (_, n, _) in enumerate(axes):
            if 2 * reach < n:
                pl.semaphore_wait(told.at[a, reach // 2], 2)

    def gather(i, unit):
        for j in far_first(nf):
            send(unit.at[own], unit.at[own], gather_send.at[i], gather_recv.at[i], on_f(j))

    gather(0, tu)
    tell(1)
    loads[1].wait()
    su[own, :] = unit_rows(sf)[0].astype(BF16)
    others = pl.ds(0, rows - local)

    loads[2].wait()
    for j in range(BLOCKS):
        values = tv[:, block(j)].astype(F32)
        inverse = 1.0 / jnp.sqrt(jnp.sum(values * values, axis=0, keepdims=True) + epsilon)
        tv[:, block(j)] = (values * inverse).astype(BF16)
    hear(1)
    tell(2)

    def student_prototypes():
        loads[3].wait()
        for j in range(BLOCKS):
            values = sv[:, block(j)].astype(F32)
            inverse = 1.0 / jnp.sqrt(jnp.sum(values * values, axis=0, keepdims=True) + epsilon)
            winv[j : j + 1, :] = inverse
            sw[:, block(j)] = (values * inverse).astype(BF16)

    def student_orders():
        each = bot // (ny * nz)
        p = lax.broadcasted_iota(jnp.int32, (bot, bot), 0)
        d = lax.broadcasted_iota(jnp.int32, (bot, bot), 1)
        pz, py, pi = p // (ny * each), lax.rem(p // each, ny), lax.rem(p, each)
        perm[...] = (d == (py * nz + pz) * each + pi).astype(F32).astype(BF16)
        for j in range(HALF, BLOCKS):
            sv[:, block(j)] = dot_nn(perm[...], sv[:, block(j)]).astype(BF16)

    def student_mass():
        took(su.at[others], gather_recv.at[1])
        units = su[...]
        p = lax.broadcasted_iota(jnp.int32, (bot, bot), 0)
        d = lax.broadcasted_iota(jnp.int32, (bot, bot), 1)
        sut[0] = dot_nt((d == p).astype(F32).astype(BF16), units).astype(BF16)
        sut[1] = dot_nt(perm[...], units).astype(BF16)
        total = jnp.zeros((rows, 128), F32)
        for j in range(BLOCKS):
            values = jnp.exp(dot_nn(su[...], sw[:, block(j)]) * (1.0 / student_temp))
            prob[j] = values
            for c in range(0, cb, 128):
                total = total + values[:, c : c + 128]
        st_own[0] = lanes_of(total)
        i = lax.broadcasted_iota(jnp.int32, (local, rows), 0)
        c = lax.broadcasted_iota(jnp.int32, (local, rows), 1)
        place = (c == f * local + i).astype(F32).astype(BF16)
        loads[4].wait()
        st_own[1] = dot_nn(cw[...], place)
        for j in far_first(nf):
            send(st_own, st_recv.at[j - 1], st_send, st_got, on_f(j))

    def col_send(it, stage, sums):
        col_own[it, stage] = sums.astype(BF16)
        axis, n, _ = axes[stage]
        for j in far_first(n):
            send(col_own.at[it, stage], col_recv.at[it, stage, j - 1], col_sent.at[it, stage], col_got.at[it, stage], axis(j))

    def col_total(it, stage):
        took(col_recv.at[it, stage], col_got.at[it, stage])
        total = col_own[it, stage].astype(F32)
        for j in range(axes[stage][1] - 1):
            total = total + col_recv[it, stage, j].astype(F32)
        return total

    hear(2)
    took(tu.at[others], gather_recv.at[0])
    for it in range(ITERS):
        for j in range(BLOCKS):
            if it == 0:
                values = jnp.exp(dot_nn(tu[...], tv[:, block(j)]) * (1.0 / teacher_temp))
                mass[j] = values
            else:
                values = mass[j] * rb[...]
            sums[j : j + 1, :] = jnp.sum(values, axis=0, keepdims=True)
        col_send(it, 0, sums[...])
        if it == 0:
            gather(1, su)
            student_prototypes()
            student_orders()
        col_send(it, 1, col_total(it, 0))
        if it == 0:
            student_mass()
        svec[...] = 1.0 / (col_total(it, 1) * protos)
        total = jnp.zeros((rows, 128), F32)
        for j in range(BLOCKS):
            values = mass[j] * svec[j : j + 1, :]
            if it == ITERS - 1:
                mass[j] = values
            for c in range(0, cb, 128):
                total = total + values[:, c : c + 128]
        row_own[it] = lanes_of(total)
        for j in far_first(nf):
            send(row_own.at[it], row_recv.at[it, j - 1], row_send.at[it], row_got.at[it], on_f(j))
        if it == ITERS - 1:
            took(st_recv, st_got)
            student_total, weights = st_own[0], st_own[1]
            for j in range(nf - 1):
                student_total = student_total + st_recv[j, 0]
                weights = weights + st_recv[j, 1]
            ab[...] = rows_of(weights / (student_total * student_temp), cb)
            for j in range(BLOCKS):
                prob[j] = prob[j] * ab[...]
        took(row_recv.at[it], row_got.at[it])
        row_total = row_own[it]
        for j in range(nf - 1):
            row_total = row_total + row_recv[it, j]
        if it < ITERS - 1:
            rb[...] = rows_of(1.0 / (row_total * crops), cb)
        else:
            bb[...] = rows_of(weights / (row_total * student_temp), cb)

    fg[...] = jnp.zeros_like(fg)
    rings = [(h, q) for q in range(PARTS) for h in range(2)]

    def chunk(h, c):
        size = bot // axes[h][1]
        return pl.ds(pl.multiple_of(c * size, size), size)

    def length(h, q, way):
        n = axes[h][1]
        return n // 2 if way == q % 2 else (n - 1) // 2

    def slot(h, q, way, far):
        return (length(h, q, 0) if way else 0) + far - 1

    def towards(h, q, way, far):
        return TOWARDS[length(h, q, way)][ROUTES[q]][far - 1]

    def senders(h, q, way, far):
        return [other for other in range(length(h, q, way), far, -1) if towards(h, q, way, other) == far]

    def depth(h, q, way, far):
        return 0 if far == 0 else 1 + depth(h, q, way, towards(h, q, way, far))

    def chain_step(h, q, way, far):
        axis, n, me = axes[h]
        r = PARTS * h + q
        rows_to = chunk(h, lax.rem(me + (far if way == 0 else n - far), n))
        for sender in senders(h, q, way, far):
            got = slot(h, q, way, sender)
            took(ring_recv.at[r, got], ring_got.at[r, got])
            part[r, rows_to, :] = part[r, rows_to, :] + ring_recv[r, got]
        hops = far - towards(h, q, way, far)
        now = slot(h, q, way, far)
        send(
            part.at[r, rows_to], ring_recv.at[r, now], ring_send.at[r], ring_got.at[r, now],
            axis(hops if way == 0 else n - hops),
        )

    def chain_steps(h, q, s):
        for way in (q % 2, 1 - q % 2):
            far_ones = range(length(h, q, way), 0, -1)
            steps = max([depth(h, q, way, far) for far in far_ones], default=0)
            for far in far_ones:
                if steps - depth(h, q, way, far) == s:
                    chain_step(h, q, way, far)

    for h, q in rings:
        r = PARTS * h + q
        for k in range(WIDE):
            j = WIDE * r + k
            g = (prob[j] - mass[j] * bb[...]).astype(BF16)
            fg[...] += dot_nt(g, sw[:, block(j)])
            grad = dot_nn(sut[h], g)
            inverse = winv[j : j + 1, :]
            w = sv[:, block(j)].astype(F32) * inverse
            inner = jnp.sum(w * grad, axis=0, keepdims=True)
            part[r, :, k * cb : (k + 1) * cb] = ((grad - w * inner) * inverse).astype(BF16)
        chain_steps(h, q, 0)

    def rows_at(i):
        return pl.ds(pl.multiple_of(i * local, local), local)

    for j in far_first(nf):
        send(fg.at[rows_at(lax.rem(f + j, nf))], fg_recv.at[j - 1], fg_send, fg_got, on_f(j))
    for s in range(1, max(ny, nz) // 2):
        for h, q in rings:
            chain_steps(h, q, s)

    each = bot // (ny * nz)
    for h in range(2):
        _, n, me = axes[h]
        totals = []
        for q in range(PARTS):
            r = PARTS * h + q
            total = part[r, chunk(h, me), :].astype(F32)
            for way in range(2):
                for sender in senders(h, q, way, 0):
                    got = slot(h, q, way, sender)
                    took(ring_recv.at[r, got], ring_got.at[r, got])
                    total = total + ring_recv[r, got].astype(F32)
            totals.append(total)
        totals = jnp.concatenate(totals, axis=1)
        totals = [totals[:, k * cb : (k + 2) * cb] for k in range(0, HALF, 2)]
        axis, n2, me2 = axes[1 - h]
        for c in range(n2):
            second[h, c] = jnp.concatenate([total[c * each : (c + 1) * each] for total in totals], axis=0).astype(BF16)
        for j in far_first(n2):
            send(second.at[h, lax.rem(me2 + j, n2)], second_recv.at[h, j - 1], second_send.at[h], second_got.at[h], axis(j))

    took(fg_recv, fg_got)
    grad = fg[rows_at(f), :]
    for j in range(nf - 1):
        grad = grad + fg_recv[j]
    hat, length = unit_rows(sf)
    gf_ref[...] = (grad - hat * jnp.sum(hat * grad, axis=1, keepdims=True)) / length

    for i, unit in enumerate((tu, su)):
        took(unit.at[others], gather_send.at[i])
    for it in range(ITERS):
        for stage in range(2):
            took(col_recv.at[it, stage], col_sent.at[it, stage])
        took(row_recv.at[it], row_send.at[it])
    took(st_recv, st_send)
    took(fg_recv, fg_send)
    for h in range(2):
        for r in range(PARTS * h, PARTS * (h + 1)):
            took(ring_recv.at[r], ring_send.at[r])

    for h in range(2):
        took(second_recv.at[h], second_got.at[h])
        _, n2, me2 = axes[1 - h]
        total = second[h, me2].astype(F32)
        for j in range(n2 - 1):
            total = total + second_recv[h, j].astype(F32)
        for q in range(4):
            first = h * HALF * cb + q * 2 * cb
            gv_ref[:, first : first + 2 * cb] = total[q * each : (q + 1) * each]
    for h in range(2):
        took(second_recv.at[h], second_send.at[h])


def hand_over(gv_ref, gf_ref, gv_out, gf_out):
    gv_out[...] = gv_ref[...]
    gf_out[...] = gf_ref[...]


def step(geo, teacher_feat, student_feat, crop_weight, teacher_v, student_v):
    ny, nz, nf = geo
    local, bot = teacher_feat.shape
    kl = teacher_v.shape[1]
    rows, cb = local * nf, kl // BLOCKS
    each = bot // (ny * nz)
    any_space = pl.BlockSpec(memory_space=pl.ANY)
    vmem = pl.BlockSpec(memory_space=pltpu.VMEM)
    dma = pltpu.SemaphoreType.DMA
    grads = pl.pallas_call(
        functools.partial(kernel, geo),
        out_shape=(
            jax.ShapeDtypeStruct((each, kl), F32),
            jax.ShapeDtypeStruct((local, bot), F32),
        ),
        in_specs=[any_space] * 5,
        out_specs=(vmem, vmem),
        scratch_shapes=[
            pltpu.VMEM((local, bot), BF16),
            pltpu.VMEM((local, bot), BF16),
            pltpu.VMEM((1, local), BF16),
            pltpu.VMEM((bot, kl), BF16),
            pltpu.VMEM((bot, kl), BF16),
            pltpu.VMEM((bot, kl), BF16),
            pltpu.VMEM((rows, bot), BF16),
            pltpu.VMEM((rows, bot), BF16),
            pltpu.VMEM((2, bot, rows), BF16),
            pltpu.VMEM((bot, bot), BF16),
            pltpu.VMEM((BLOCKS, rows, cb), F32),
            pltpu.VMEM((BLOCKS, rows, cb), F32),
            pltpu.VMEM((BLOCKS, cb), F32),
            pltpu.VMEM((BLOCKS, cb), F32),
            pltpu.VMEM((rows, cb), F32),
            pltpu.VMEM((rows, cb), F32),
            pltpu.VMEM((rows, cb), F32),
            pltpu.VMEM((rows, bot), F32),
            pltpu.VMEM((BLOCKS, cb), F32),
            pltpu.VMEM((ITERS, 2, BLOCKS, cb), BF16),
            pltpu.VMEM((ITERS, 2, ny - 1, BLOCKS, cb), BF16),
            pltpu.VMEM((ITERS, 1, rows), F32),
            pltpu.VMEM((ITERS, nf - 1, 1, rows), F32),
            pltpu.VMEM((2, 1, rows), F32),
            pltpu.VMEM((nf - 1, 2, 1, rows), F32),
            pltpu.VMEM((2 * PARTS, bot, WIDE * cb), BF16),
            pltpu.VMEM((2 * PARTS, ny - 1, bot // ny, WIDE * cb), BF16),
            pltpu.VMEM((2, ny, 4 * each, 2 * cb), BF16),
            pltpu.VMEM((2, ny - 1, 4 * each, 2 * cb), BF16),
            pltpu.VMEM((nf - 1, local, bot), F32),
            pltpu.SemaphoreType.REGULAR((2, 2)),
            dma((5,)),
            dma((2,)), dma((2,)),
            dma((ITERS, 2)), dma((ITERS, 2)),
            dma((ITERS,)), dma((ITERS,)),
            dma, dma,
            dma((2 * PARTS,)), dma((2 * PARTS, ny - 1)),
            dma((2,)), dma((2,)),
            dma, dma,
        ],
        compiler_params=pltpu.CompilerParams(
            collective_id=0, has_side_effects=True, vmem_limit_bytes=62 * 1024 * 1024
        ),
    )(teacher_feat, student_feat, crop_weight.reshape(1, local), teacher_v, student_v)
    return pl.pallas_call(
        hand_over,
        out_shape=[jax.ShapeDtypeStruct(grad.shape, grad.dtype) for grad in grads],
        in_specs=[vmem, vmem],
        out_specs=[vmem, vmem],
    )(*grads)


def solution(mesh, planes=(8, 8)):
    geo = (*planes, mesh.shape["fsdp"])
    placed = (
        P(("dp", "fsdp"), None),
        P(("dp", "fsdp"), None),
        P(("dp", "fsdp")),
        P(None, "fsdp"),
        P(None, "fsdp"),
    )
    return jax.shard_map(
        functools.partial(step, geo),
        mesh=mesh,
        in_specs=placed,
        out_specs=(P("dp", "fsdp"), P(("dp", "fsdp"), None)),
        check_vma=False,
    )
```
